32 devices in a mesh: blk: 16 (over z, x, core), span: 2 (over y).
Axes of the slice: x: 2, y: 2, z: 4, core: 2. Of those that a mesh axis runs over, the one named last changes fastest.
Arguments:
- state_now: float32 [5, 9, 16, 256, 128], P(None, None, 'span', 'blk'), may hold values from -6 to 6
- base_state: float32 [5, 9, 16, 256, 128], P(None, None, 'span', 'blk'), may hold values from -6 to 6
- time_step: float32 [16, 256, 128], P('span', 'blk'), may hold values from 0.05 to 0.3
- row_map: int32 [16], replicated, may hold values from 0 to 2, as said below
- lag_shift: int32 [3], replicated, may hold values from 1 to 8
- mode_count: int32 [2], replicated, may hold values from 8 to 16, as said below
- jacobian: float32 [3, 3, 5, 5], replicated, may hold values from -2.5 to 2.5
- dissipation: float32 [3, 3], replicated, may hold values from 0.2 to 1
- frequency: float32 [3], replicated, may hold values from 0.5 to 2
Outputs:
- state_next: float32 [5, 9, 16, 256, 128], P(None, None, 'span', 'blk')
The draws below stay inside these ranges and needn't reach their ends.
Inputs may be any that keep to these rules, and one draw needn't show every extreme that they name: `row_map`: never falling; the 3 rows hold 2, 9 and the remaining blocks, in an order that varies. `mode_count`: one interface keeps exactly 16 modes.
All inputs are finite; a program needn't handle non-finite values.
Results may differ from the reference program's by a relative error of at most 0.00005.
Values sent between devices are 32-bit elements; how exact they have to be, the bound alone decides.
A program may use at most 192 MiB of HBM per device.

```python
import math
import jax
import jax.numpy as jnp
from jax import lax

VARS = 5
INST = 9
ROWS = 3
MODES = 16
PCH = 16
AX = 128
NP = 256
SPAN = 16
N_BLK = 16


def draw_row_map(key, part):
    widest = N_BLK // 2 + 1
    lengths = jnp.array([2, widest, N_BLK - widest - 2], dtype=jnp.int32)
    order = jax.random.permutation(jax.random.fold_in(key, 11), ROWS)
    counts = lengths[order]
    ends = jnp.cumsum(counts)
    block_ids = jnp.arange(N_BLK, dtype=jnp.int32)
    return jnp.sum((block_ids[:, None] >= ends[None, :]).astype(jnp.int32), axis=1).astype(jnp.int32)


def draw_mode_count(key, part):
    lower = jax.random.randint(jax.random.fold_in(key, 23), (ROWS - 1,), MODES // 2, MODES)
    chosen = jax.random.randint(jax.random.fold_in(key, 29), (), 0, ROWS - 1)
    return jnp.where(jnp.arange(ROWS - 1, dtype=jnp.int32) == chosen, MODES, lower).astype(jnp.int32)


def shard_levels(rng, shape, cuts, low, high):
    loudness, own = 1.0, jax.random.fold_in(rng, 6)
    for axis_at, parts in cuts:
        draws = jnp.exp(jax.random.uniform(jax.random.fold_in(own, axis_at), (parts,), jnp.float32, low / len(cuts), high / len(cuts)))
        loudness = loudness * jnp.repeat(draws, shape[axis_at] // parts).reshape([-1 if axis == axis_at else 1 for axis in range(len(shape))])
    return loudness


def scatter_about(stream_key, extent, deviation, reach, pieces=(), held_as=jnp.bfloat16):
    values = deviation * jax.random.normal(stream_key, extent, jnp.float32)
    if pieces:
        values = values * shard_levels(stream_key, extent, pieces, -0.22, 0.18)
    return jnp.clip(values, -reach, reach).astype(held_as)


def setup_inputs(seed: int = 0) -> dict:
    seeds = jax.random.split(jax.random.key(seed), 10)
    state_now = scatter_about(seeds[0], (VARS, INST, SPAN, NP, AX), 1.0, 6.0, ((2, 2), (3, 16)), jnp.float32)
    base_state = scatter_about(seeds[1], (VARS, INST, SPAN, NP, AX), 1.0, 6.0, ((2, 2), (3, 16)), jnp.float32)
    time_step = jnp.clip(jnp.exp(math.log(0.3) - 1.7917595 * jax.random.uniform(seeds[2], (SPAN, NP, AX), jnp.float32) ** shard_levels(seeds[2], (SPAN, NP, AX), ((0, 2), (1, 16)), -0.2, 0.2)), 0.05, 0.3)
    row_map = draw_row_map(jax.random.fold_in(seeds[9], 71), 0)
    lag_shift = jax.random.randint(seeds[4], (ROWS,), 1, INST).astype(jnp.int32)
    mode_count = draw_mode_count(jax.random.fold_in(seeds[9], 71), 0)
    jacobian = scatter_about(seeds[6], (ROWS, 3, VARS, VARS), VARS ** -0.5, 2.5, (), jnp.float32)
    dissipation = jnp.clip(jnp.exp(jax.random.uniform(seeds[7], (ROWS, 3), jnp.float32, math.log(0.2), math.log(1.0))), 0.2, 1.0)
    frequency = jnp.clip(jnp.exp(jax.random.uniform(seeds[8], (ROWS,), jnp.float32, math.log(0.5), math.log(2.0))), 0.5, 2.0)
    return {"state_now": state_now, "base_state": base_state, "time_step": time_step, "row_map": row_map, "lag_shift": lag_shift, "mode_count": mode_count, "jacobian": jacobian, "dissipation": dissipation, "frequency": frequency}


def spectral_table():
    row_ids = jnp.arange(INST, dtype=jnp.int32)[:, None]
    col_ids = jnp.arange(INST, dtype=jnp.int32)[None, :]
    offset = (row_ids - col_ids).astype(jnp.float32)
    on_diagonal = row_ids == col_ids
    denominator = jnp.where(on_diagonal, jnp.float32(1.0), jnp.sin(jnp.pi * offset / INST))
    return jnp.where(on_diagonal, jnp.float32(0.0), 0.5 * jnp.cos(jnp.pi * offset) / denominator)


def roll_table(shifts):
    source = (jnp.arange(INST, dtype=jnp.int32)[:, None] + shifts[None, :]) % INST
    return (source[:, None, :] == jnp.arange(INST, dtype=jnp.int32)[None, :, None]).astype(jnp.float32)


def reference(state_now, base_state, time_step, row_map, lag_shift, mode_count, jacobian, dissipation, frequency):
    exact = lax.Precision.HIGHEST
    columns = state_now.shape[3]
    axial = state_now.shape[4]
    col_ids = jnp.arange(columns, dtype=jnp.int32)
    row_ids = jnp.arange(ROWS, dtype=jnp.int32)
    column_row = row_map[col_ids // PCH]
    row_hot = (row_ids[:, None] == column_row[None, :]).astype(jnp.float32)
    block_total = jnp.sum((row_map[None, :] == row_ids[:, None]).astype(jnp.int32), axis=1)
    block_begin = jnp.cumsum(block_total) - block_total
    column_begin = block_begin[column_row] * PCH
    column_width = block_total[column_row] * PCH
    column_final = column_begin + column_width - 1
    left_index = jnp.where(col_ids > column_begin, col_ids - 1, column_final)
    right_index = jnp.where(col_ids < column_final, col_ids + 1, column_begin)
    column_lag = lag_shift[column_row]
    left_shift = jnp.where(col_ids == column_begin, column_lag, 0).astype(jnp.int32)
    right_shift = jnp.where(col_ids == column_final, -column_lag, 0).astype(jnp.int32)
    left_field = jnp.einsum('vksca,jkc->vjsca', jnp.take(state_now, left_index, axis=3), roll_table(left_shift), precision=exact)
    right_field = jnp.einsum('vksca,jkc->vjsca', jnp.take(state_now, right_index, axis=3), roll_table(right_shift), precision=exact)
    span_pad = jnp.pad(state_now, ((0, 0), (0, 0), (1, 1), (0, 0), (0, 0)))
    mode_ids = jnp.arange(MODES, dtype=jnp.int32)
    circle = column_width.astype(jnp.float32)
    angle = 2.0 * jnp.pi * ((col_ids - column_begin).astype(jnp.float32) + 0.5) / circle
    harmonic = mode_ids.astype(jnp.float32)[:, None] * angle[None, :]
    cos_basis = jnp.cos(harmonic)
    sin_basis = jnp.sin(harmonic)
    mode_weight = jnp.where(mode_ids == 0, 1.0, 2.0).astype(jnp.float32)[:, None] / circle[None, :]

    def project(face):
        cosine = jnp.einsum('vksc,mc,rc->rvksm', face, cos_basis * mode_weight, row_hot, precision=exact)
        sine = jnp.einsum('vksc,mc,rc->rvksm', face, sin_basis * mode_weight, row_hot, precision=exact)
        return cosine, sine

    outlet_cos, outlet_sin = project(state_now[..., axial - 1])
    inlet_cos, inlet_sin = project(state_now[..., 0])
    previous_hot = (row_ids[:, None] == column_row[None, :] - 1).astype(jnp.float32)
    next_hot = (row_ids[:, None] == column_row[None, :] + 1).astype(jnp.float32)
    inlet_limit = mode_count[jnp.clip(column_row - 1, 0, ROWS - 2)]
    outlet_limit = mode_count[jnp.clip(column_row, 0, ROWS - 2)]
    inlet_mask = (mode_ids[:, None] < inlet_limit[None, :]).astype(jnp.float32)
    outlet_mask = (mode_ids[:, None] < outlet_limit[None, :]).astype(jnp.float32)
    ghost_in = jnp.einsum('rvksm,rc,mc->vksc', outlet_cos, previous_hot, cos_basis * inlet_mask, precision=exact)
    ghost_in = ghost_in + jnp.einsum('rvksm,rc,mc->vksc', outlet_sin, previous_hot, sin_basis * inlet_mask, precision=exact)
    ghost_out = jnp.einsum('rvksm,rc,mc->vksc', inlet_cos, next_hot, cos_basis * outlet_mask, precision=exact)
    ghost_out = ghost_out + jnp.einsum('rvksm,rc,mc->vksc', inlet_sin, next_hot, sin_basis * outlet_mask, precision=exact)
    axial_pad = jnp.concatenate([ghost_in[..., None], state_now, ghost_out[..., None]], axis=4)
    column_jac = jacobian[column_row]
    column_dissip = dissipation[column_row]

    def direction_term(plus, minus, number):
        flux = 0.5 * jnp.einsum('cuv,vksca->uksca', column_jac[:, number], plus - minus, precision=exact)
        return flux - column_dissip[:, number][None, None, None, :, None] * (plus - 2.0 * state_now + minus)

    residual = direction_term(right_field, left_field, 0)
    residual = residual + direction_term(axial_pad[..., 2:], axial_pad[..., :-2], 1)
    residual = residual + direction_term(span_pad[:, :, 2:], span_pad[:, :, :-2], 2)
    spectral = frequency[column_row][None, None, None, :, None] * jnp.einsum('jk,vksca->vjsca', spectral_table(), state_now, precision=exact)
    return base_state - time_step[None, None] * (residual + spectral)
```

```python
import functools
import itertools

import jax
import jax.numpy as jnp
import numpy as np
from jax import lax
from jax.experimental import pallas as pl
from jax.experimental.pallas import tpu as pltpu
from jax.sharding import PartitionSpec as P

MODES = 16
MESH_ID = pl.DeviceIdType.MESH


def row_orders(blocks):
    widest = blocks // 2 + 1
    lengths = (2, widest, blocks - widest - 2)
    return lengths, [tuple(lengths[i] for i in order) for order in itertools.permutations(range(3))]


def mode_tables(blocks, pitch):
    _, orders = row_orders(blocks)
    columns = blocks * pitch
    modes = np.arange(MODES)
    weight = np.where(modes == 0, 1.0, 2.0)
    analysis = np.zeros((len(orders), 2, 2, 2, MODES, columns))
    synthesis = np.zeros((len(orders), 2, 2, 2, MODES, columns))
    for number, counts in enumerate(orders):
        begin = 0
        for row, count in enumerate(counts):
            width = count * pitch
            own = slice(begin, begin + width)
            phase = modes[:, None] * (2.0 * np.pi * (np.arange(width) + 0.5) / width)[None, :]
            basis = np.stack([np.cos(phase), np.sin(phase)])
            scaled = basis * weight[None, :, None] / width
            if row < 2:
                analysis[number, 0, row, :, :, own] = scaled
                synthesis[number, 1, row, :, :, own] = basis
            if row > 0:
                analysis[number, 1, row - 1, :, :, own] = scaled
                synthesis[number, 0, row - 1, :, :, own] = basis
            begin += width
    analysis = analysis.reshape(len(orders), 8 * MODES, columns)
    synthesis = synthesis.reshape(len(orders), 8 * MODES, columns).transpose(0, 2, 1)
    return analysis.astype(np.float32), synthesis.astype(np.float32)


def circulant(instances):
    offsets = np.arange(1, instances // 2 + 1)
    return [float(x) for x in 0.5 * np.cos(np.pi * offsets) / np.sin(np.pi * offsets / instances)]


def kernel(
    n_blk,
    state_hbm,
    base_hbm,
    step_hbm,
    row_map,
    lag_shift,
    mode_count,
    jacobian,
    dissipation,
    frequency,
    analysis,
    synthesis,
    out_hbm,
    cells,
    result,
    step,
    rims,
    left_buf,
    right_buf,
    faces,
    gathered,
    spread,
    ghosts,
    load_sem,
    span_sem,
    left_send,
    left_recv,
    right_send,
    right_recv,
    face_send,
    face_recv,
    ghost_send,
    ghost_recv,
    out_sem,
):
    variables, instances, span_cells, pitch, axial = state_hbm.shape
    lengths, orders = row_orders(n_blk)
    stride = n_blk // span_cells
    blk = lax.axis_index("blk")
    span = lax.axis_index("span")

    load_state = pltpu.make_async_copy(
        state_hbm, cells.at[:, :, pl.ds(1, span_cells)], load_sem.at[0]
    )
    load_base = pltpu.make_async_copy(base_hbm, result, load_sem.at[1])
    load_step = pltpu.make_async_copy(step_hbm, step, load_sem.at[2])
    load_state.start()
    load_base.start()
    load_step.start()

    barrier = pltpu.get_barrier_semaphore()
    pl.semaphore_signal(barrier, inc=1, device_id=(blk, 1 - span), device_id_type=MESH_ID)

    def greet(d, carry):
        other = lax.rem(blk + d, n_blk)
        pl.semaphore_signal(barrier, inc=1, device_id=(other, span), device_id_type=MESH_ID)
        return carry

    lax.fori_loop(1, n_blk, greet, 0)

    sub = lax.broadcasted_iota(jnp.int32, (pitch, axial), 0)
    lane = lax.broadcasted_iota(jnp.int32, (pitch, axial), 1)
    pair = lane // 2

    def clear(k, carry):
        for v in range(variables):
            cells[v, k, (span_cells + 1) * span] = jnp.zeros((pitch, axial), jnp.float32)
        return carry

    lax.fori_loop(0, instances, clear, 0)

    pl.semaphore_wait(barrier, n_blk)
    span_copy = pltpu.make_async_remote_copy(
        src_ref=state_hbm.at[:, :, (span_cells - 1) * (1 - span)],
        dst_ref=cells.at[:, :, (span_cells + 1) * span],
        send_sem=span_sem.at[0],
        recv_sem=span_sem.at[1],
        device_id=(blk, 1 - span),
        device_id_type=MESH_ID,
    )

    load_state.wait()

    def take_layer(s, carry):
        def take(k, tile):
            for v in range(variables):
                n = v * instances + k
                moved = pltpu.roll(cells[v, k, s + 1], 2 * n + 1, 1)
                tile = jnp.where(pair == n, moved, tile)
            return tile

        faces[s] = lax.fori_loop(0, instances, take, jnp.zeros((pitch, axial), jnp.float32))
        owner = s * stride

        @pl.when(blk == owner)
        def _():
            gathered[blk] = faces[s]

        @pl.when(blk != owner)
        def _():
            pltpu.make_async_remote_copy(
                src_ref=faces.at[s],
                dst_ref=gathered.at[blk],
                send_sem=face_send.at[s],
                recv_sem=face_recv.at[blk],
                device_id=(owner, span),
                device_id_type=MESH_ID,
            ).start()

        return carry

    lax.fori_loop(0, span_cells, take_layer, 0)
    span_copy.start()

    def pack(k, carry):
        for v in range(variables):
            rims[0, v, k] = cells[v, k, pl.ds(1, span_cells), 0, :]
            rims[1, v, k] = cells[v, k, pl.ds(1, span_cells), pitch - 1, :]
        return carry

    lax.fori_loop(0, instances, pack, 0)

    def rim_copy(side, slot, distance):
        other = blk + distance
        buf, send, recv = (
            (right_buf, right_send, right_recv) if side == 0 else (left_buf, left_send, left_recv)
        )
        return pltpu.make_async_remote_copy(
            src_ref=rims.at[side],
            dst_ref=buf.at[slot],
            send_sem=send.at[slot],
            recv_sem=recv.at[slot],
            device_id=(other, span),
            device_id_type=MESH_ID,
        )

    def any_of(values):
        hit = blk == values[0]
        for value in values[1:]:
            hit = hit | (blk == value)
        return hit

    transfers = [
        (blk < n_blk - 1, blk > 0, 1, 0, 1),
        (blk > 0, blk < n_blk - 1, 0, 0, -1),
    ]
    for number, count in enumerate(lengths):
        begins = sorted({sum(o[: o.index(count)]) for o in orders})
        is_begin = any_of(begins)
        is_end = any_of([b + count - 1 for b in begins])
        transfers.append((is_end, is_begin, 1, number + 1, -(count - 1)))
        transfers.append((is_begin, is_end, 0, number + 1, count - 1))
    for sends, _, side, slot, distance in transfers:

        @pl.when(sends)
        def _(side=side, slot=slot, distance=distance):
            rim_copy(side, slot, distance).start()

    counts = [0, 0, 0]
    for b in range(n_blk):
        for r in range(3):
            counts[r] = counts[r] + (row_map[b] == r).astype(jnp.int32)
    order = jnp.int32(0)
    for number, o in enumerate(orders):
        same = (counts[0] == o[0]) & (counts[1] == o[1])
        order = order + jnp.where(same, number, 0)
    own_row = row_map[blk]
    own_count = jnp.where(own_row == 0, counts[0], jnp.where(own_row == 1, counts[1], counts[2]))
    own_begin = jnp.where(
        own_row == 0, 0, jnp.where(own_row == 1, counts[0], counts[0] + counts[1])
    )
    at_begin = blk == own_begin
    at_final = blk == own_begin + own_count - 1
    wrap_slot = jnp.where(
        own_count == lengths[0], 1, jnp.where(own_count == lengths[1], 2, 3)
    )
    lag = lag_shift[own_row]
    left_slot = jnp.where(at_begin, wrap_slot, 0)
    right_slot = jnp.where(at_final, wrap_slot, 0)
    left_lag = jnp.where(at_begin, lag, 0)
    right_lag = jnp.where(at_final, instances - lag, 0)

    def others(body):
        def turn(d, carry):
            body(lax.rem(blk + d, n_blk))
            return carry

        lax.fori_loop(1, n_blk, turn, 0)

    def ghost_copy(s, other):
        return pltpu.make_async_remote_copy(
            src_ref=spread.at[other],
            dst_ref=ghosts.at[s],
            send_sem=ghost_send.at[other],
            recv_sem=ghost_recv.at[s],
            device_id=(other, span),
            device_id_type=MESH_ID,
        )

    def face_copy(s, source):
        return pltpu.make_async_remote_copy(
            src_ref=faces.at[s],
            dst_ref=gathered.at[source],
            send_sem=face_send.at[s],
            recv_sem=face_recv.at[source],
            device_id=(source, span),
            device_id_type=MESH_ID,
        )

    own_layer = blk // stride
    is_owner = blk == own_layer * stride

    @pl.when(is_owner)
    def _():
        others(lambda other: face_copy(own_layer, other).wait_recv())
        columns = gathered[...].reshape(n_blk * pitch, axial)
        coefs = jnp.dot(
            analysis[order],
            columns,
            precision=lax.Precision.HIGHEST,
            preferred_element_type=jnp.float32,
        )
        shape = coefs.shape
        term = lax.broadcasted_iota(jnp.int32, shape, 0)
        spot = lax.broadcasted_iota(jnp.int32, shape, 1)
        limit = jnp.where((term // 32) % 2 == 0, mode_count[0], mode_count[1])
        keep = ((term % MODES) < limit) & ((term // 64) == (spot % 2))
        coefs = jnp.where(keep, coefs, 0.0)
        coefs = jnp.where(spot % 2 == 0, pltpu.roll(coefs, axial - 1, 1), pltpu.roll(coefs, 1, 1))
        values = jnp.dot(
            synthesis[order],
            coefs,
            precision=lax.Precision.HIGHEST,
            preferred_element_type=jnp.float32,
        )
        spread[...] = values.reshape(n_blk, pitch, axial)
        ghosts[own_layer] = spread[blk]
        others(lambda other: ghost_copy(own_layer, other).start())

    load_base.wait()
    load_step.wait()
    for _, receives, side, slot, distance in transfers:

        @pl.when(receives)
        def _(side=side, slot=slot, distance=distance):
            rim_copy(side, slot, -distance).wait_recv()

    def each_layer(body):
        def turn(s, carry):
            body(s)
            return carry

        lax.fori_loop(0, span_cells, turn, 0)

    def wait_ghost(s):
        @pl.when(blk != s * stride)
        def _():
            ghost_copy(s, s * stride).wait_recv()

    each_layer(wait_ghost)

    table = circulant(instances)
    freq = frequency[own_row]
    spectral_weights = [freq * w for w in table]
    damping = [dissipation[own_row, d] for d in range(3)]
    centre = 2.0 * (damping[0] + damping[1] + damping[2])

    def out_copy(s):
        return pltpu.make_async_copy(result.at[:, :, s], out_hbm.at[:, :, s], out_sem.at[s])

    def layer(t, carry):
        s = (span_cells - 1) * span + t * (1 - 2 * span)

        def instant(k, inner):
            k_left = lax.rem(k + left_lag, instances)
            k_right = lax.rem(k + right_lag, instances)
            near = ghosts[s]
            before = [lax.rem(k + instances - n, instances) for n in range(1, instances // 2 + 1)]
            after = [lax.rem(k + n, instances) for n in range(1, instances // 2 + 1)]
            total, differences = [], []
            for v in range(variables):
                here = cells[v, k, s + 1]
                ghost = pltpu.roll(near, lax.rem(255 - 2 * (v * instances + k), 128), 1)
                left = left_buf[left_slot, v, k_left, pl.ds(s, 1), :]
                right = right_buf[right_slot, v, k_right, pl.ds(s, 1), :]
                minus = [
                    jnp.where(sub == 0, left, pltpu.roll(here, 1, 0)),
                    jnp.where(lane == 0, ghost, pltpu.roll(here, 1, 1)),
                    cells[v, k, s],
                ]
                plus = [
                    jnp.where(sub == pitch - 1, right, pltpu.roll(here, pitch - 1, 0)),
                    jnp.where(lane == axial - 1, ghost, pltpu.roll(here, axial - 1, 1)),
                    cells[v, k, s + 2],
                ]
                differences.append([plus[d] - minus[d] for d in range(3)])
                value = centre * here
                for d in range(3):
                    value = value - damping[d] * (plus[d] + minus[d])
                for n, weight in enumerate(spectral_weights):
                    value = value + weight * (
                        cells[v, before[n], s + 1] - cells[v, after[n], s + 1]
                    )
                total.append(value)
            pace = step[s]
            for u in range(variables):
                value = total[u]
                for d in range(3):
                    for v in range(variables):
                        value = value + (0.5 * jacobian[own_row, d, u, v]) * differences[v][d]
                result[u, k, s] = result[u, k, s] - pace * value
            return inner

        lax.fori_loop(0, instances, instant, 0)
        out_copy(s).start()
        return carry

    lax.fori_loop(0, span_cells - 1, layer, 0)
    span_copy.wait_recv()
    lax.fori_loop(span_cells - 1, span_cells, layer, 0)

    span_copy.wait_send()
    for sends, _, side, slot, distance in transfers:

        @pl.when(sends)
        def _(side=side, slot=slot, distance=distance):
            rim_copy(side, slot, distance).wait_send()

    def wait_face(s):
        @pl.when(blk != s * stride)
        def _():
            face_copy(s, s * stride).wait_send()

    each_layer(wait_face)

    @pl.when(is_owner)
    def _():
        others(lambda other: ghost_copy(own_layer, other).wait_send())

    each_layer(lambda s: out_copy(s).wait())


def per_device(n_blk, *arrays):
    state_now = arrays[0]
    variables, instances, span_cells, pitch, axial = state_now.shape
    analysis, synthesis = mode_tables(n_blk, pitch)
    anywhere = pl.BlockSpec(memory_space=pl.ANY)
    scalars = pl.BlockSpec(memory_space=pltpu.SMEM)
    vector = pl.BlockSpec(memory_space=pltpu.VMEM)
    f32 = jnp.float32
    dma = pltpu.SemaphoreType.DMA
    return pl.pallas_call(
        functools.partial(kernel, n_blk),
        out_shape=jax.ShapeDtypeStruct(state_now.shape, f32),
        in_specs=[anywhere] * 3 + [scalars] * 6 + [vector] * 2,
        out_specs=anywhere,
        scratch_shapes=[
            pltpu.VMEM((variables, instances, span_cells + 2, pitch, axial), f32),
            pltpu.VMEM(state_now.shape, f32),
            pltpu.VMEM((span_cells, pitch, axial), f32),
            pltpu.VMEM((2, variables, instances, span_cells, axial), f32),
            pltpu.VMEM((4, variables, instances, span_cells, axial), f32),
            pltpu.VMEM((4, variables, instances, span_cells, axial), f32),
            pltpu.VMEM((span_cells, pitch, axial), f32),
            pltpu.VMEM((n_blk, pitch, axial), f32),
            pltpu.VMEM((n_blk, pitch, axial), f32),
            pltpu.VMEM((span_cells, pitch, axial), f32),
            dma((3,)),
            dma((2,)),
            dma((4,)),
            dma((4,)),
            dma((4,)),
            dma((4,)),
            dma((span_cells,)),
            dma((n_blk,)),
            dma((n_blk,)),
            dma((span_cells,)),
            dma((span_cells,)),
        ],
        compiler_params=pltpu.CompilerParams(
            collective_id=0, has_side_effects=True, vmem_limit_bytes=32 * 1024 * 1024
        ),
    )(*arrays, analysis, synthesis)


def solution(mesh):
    return jax.shard_map(
        functools.partial(per_device, mesh.shape["blk"]),
        mesh=mesh,
        in_specs=(
            P(None, None, "span", "blk", None),
            P(None, None, "span", "blk", None),
            P("span", "blk", None),
            P(),
            P(),
            P(),
            P(),
            P(),
            P(),
        ),
        out_specs=P(None, None, "span", "blk", None),
        check_vma=False,
    )
```

```python
import functools
import itertools

import jax
import jax.numpy as jnp
import numpy as np
from jax import lax
from jax.experimental import pallas as pl
from jax.experimental.pallas import tpu as pltpu
from jax.sharding import PartitionSpec as P

MODES = 16
MESH_ID = pl.DeviceIdType.MESH


def row_orders(blocks):
    widest = blocks // 2 + 1
    lengths = (2, widest, blocks - widest - 2)
    return lengths, [tuple(lengths[i] for i in order) for order in itertools.permutations(range(3))]


def mode_tables(blocks, pitch):
    _, orders = row_orders(blocks)
    columns = blocks * pitch
    modes = np.arange(MODES)
    weight = np.where(modes == 0, 1.0, 2.0)
    analysis = np.zeros((len(orders), 2, 2, 2, MODES, columns))
    synthesis = np.zeros((len(orders), 2, 2, 2, MODES, columns))
    for number, counts in enumerate(orders):
        begin = 0
        for row, count in enumerate(counts):
            width = count * pitch
            own = slice(begin, begin + width)
            phase = modes[:, None] * (2.0 * np.pi * (np.arange(width) + 0.5) / width)[None, :]
            basis = np.stack([np.cos(phase), np.sin(phase)])
            scaled = basis * weight[None, :, None] / width
            if row < 2:
                analysis[number, 0, row, :, :, own] = scaled
                synthesis[number, 1, row, :, :, own] = basis
            if row > 0:
                analysis[number, 1, row - 1, :, :, own] = scaled
                synthesis[number, 0, row - 1, :, :, own] = basis
            begin += width
    analysis = analysis.reshape(len(orders), 8 * MODES, columns)
    synthesis = synthesis.reshape(len(orders), 8 * MODES, columns).transpose(0, 2, 1)
    return analysis.astype(np.float32), synthesis.astype(np.float32)


def circulant(instances):
    offsets = np.arange(1, instances // 2 + 1)
    return [float(x) for x in 0.5 * np.cos(np.pi * offsets) / np.sin(np.pi * offsets / instances)]


def kernel(
    n_blk,
    state_hbm,
    base_hbm,
    step_hbm,
    row_map_hbm,
    lag_shift_hbm,
    mode_count_hbm,
    jacobian_hbm,
    dissipation_hbm,
    frequency_hbm,
    analysis_hbm,
    synthesis_hbm,
    out_hbm,
    cells,
    result,
    step,
    rims,
    left_buf,
    right_buf,
    faces,
    gathered,
    spread,
    ghosts,
    row_map,
    lag_shift,
    mode_count,
    jacobian,
    dissipation,
    frequency,
    analysis,
    synthesis,
    load_sem,
    span_sem,
    left_send,
    left_recv,
    right_send,
    right_recv,
    face_send,
    face_recv,
    ghost_send,
    ghost_recv,
    out_sem,
):
    variables, instances, span_cells, pitch, axial = state_hbm.shape
    lengths, orders = row_orders(n_blk)
    stride = n_blk // span_cells
    blk = lax.axis_index("blk")
    span = lax.axis_index("span")

    load_state = pltpu.make_async_copy(
        state_hbm, cells.at[:, :, pl.ds(1, span_cells)], load_sem.at[0]
    )
    load_base = pltpu.make_async_copy(base_hbm, result, load_sem.at[1])
    load_step = pltpu.make_async_copy(step_hbm, step, load_sem.at[2])
    load_state.start()
    load_base.start()
    load_step.start()
    pairs = [
        (row_map_hbm, row_map),
        (lag_shift_hbm, lag_shift),
        (mode_count_hbm, mode_count),
        (jacobian_hbm, jacobian),
        (dissipation_hbm, dissipation),
        (frequency_hbm, frequency),
        (analysis_hbm, analysis),
        (synthesis_hbm, synthesis),
    ]
    load_rest = [
        pltpu.make_async_copy(source, target, load_sem.at[3 + i])
        for i, (source, target) in enumerate(pairs)
    ]
    for load in load_rest:
        load.start()

    barrier = pltpu.get_barrier_semaphore()
    pl.semaphore_signal(barrier, inc=1, device_id=(blk, 1 - span), device_id_type=MESH_ID)

    def greet(d, carry):
        other = lax.rem(blk + d, n_blk)
        pl.semaphore_signal(barrier, inc=1, device_id=(other, span), device_id_type=MESH_ID)
        return carry

    lax.fori_loop(1, n_blk, greet, 0)

    sub = lax.broadcasted_iota(jnp.int32, (pitch, axial), 0)
    lane = lax.broadcasted_iota(jnp.int32, (pitch, axial), 1)
    pair = lane // 2

    def clear(k, carry):
        for v in range(variables):
            cells[v, k, (span_cells + 1) * span] = jnp.zeros((pitch, axial), jnp.float32)
        return carry

    lax.fori_loop(0, instances, clear, 0)

    span_copy = pltpu.make_async_remote_copy(
        src_ref=state_hbm.at[:, :, (span_cells - 1) * (1 - span)],
        dst_ref=cells.at[:, :, (span_cells + 1) * span],
        send_sem=span_sem.at[0],
        recv_sem=span_sem.at[1],
        device_id=(blk, 1 - span),
        device_id_type=MESH_ID,
    )

    load_state.wait()

    def take(k, tiles):
        tiles = list(tiles)
        for v in range(variables):
            n = v * instances + k
            chosen = pair == n
            for s in range(span_cells):
                tiles[s] = jnp.where(chosen, pltpu.roll(cells[v, k, s + 1], 2 * n + 1, 1), tiles[s])
        return tuple(tiles)

    blank = jnp.zeros((pitch, axial), jnp.float32)
    for s, tile in enumerate(lax.fori_loop(0, instances, take, (blank,) * span_cells)):
        faces[s] = tile

    pl.semaphore_wait(barrier, n_blk)

    def send_layer(s, carry):
        owner = s * stride

        @pl.when(blk == owner)
        def _():
            gathered[blk] = faces[s]

        @pl.when(blk != owner)
        def _():
            pltpu.make_async_remote_copy(
                src_ref=faces.at[s],
                dst_ref=gathered.at[blk],
                send_sem=face_send.at[s],
                recv_sem=face_recv.at[blk],
                device_id=(owner, span),
                device_id_type=MESH_ID,
            ).start()

        return carry

    lax.fori_loop(0, span_cells, send_layer, 0)
    span_copy.start()

    def pack(k, carry):
        for v in range(variables):
            rims[0, v, k] = cells[v, k, pl.ds(1, span_cells), 0, :]
            rims[1, v, k] = cells[v, k, pl.ds(1, span_cells), pitch - 1, :]
        return carry

    lax.fori_loop(0, instances, pack, 0)

    def rim_copy(side, slot, distance):
        other = blk + distance
        buf, send, recv = (
            (right_buf, right_send, right_recv) if side == 0 else (left_buf, left_send, left_recv)
        )
        return pltpu.make_async_remote_copy(
            src_ref=rims.at[side],
            dst_ref=buf.at[slot],
            send_sem=send.at[slot],
            recv_sem=recv.at[slot],
            device_id=(other, span),
            device_id_type=MESH_ID,
        )

    def any_of(values):
        hit = blk == values[0]
        for value in values[1:]:
            hit = hit | (blk == value)
        return hit

    transfers = [
        (blk < n_blk - 1, blk > 0, 1, 0, 1),
        (blk > 0, blk < n_blk - 1, 0, 0, -1),
    ]
    for number, count in enumerate(lengths):
        begins = sorted({sum(o[: o.index(count)]) for o in orders})
        is_begin = any_of(begins)
        is_end = any_of([b + count - 1 for b in begins])
        transfers.append((is_end, is_begin, 1, number + 1, -(count - 1)))
        transfers.append((is_begin, is_end, 0, number + 1, count - 1))
    for sends, _, side, slot, distance in transfers:

        @pl.when(sends)
        def _(side=side, slot=slot, distance=distance):
            rim_copy(side, slot, distance).start()

    for load in load_rest:
        load.wait()

    counts = [0, 0, 0]
    for b in range(n_blk):
        for r in range(3):
            counts[r] = counts[r] + (row_map[b] == r).astype(jnp.int32)
    order = jnp.int32(0)
    for number, o in enumerate(orders):
        same = (counts[0] == o[0]) & (counts[1] == o[1])
        order = order + jnp.where(same, number, 0)
    own_row = row_map[blk]
    own_count = jnp.where(own_row == 0, counts[0], jnp.where(own_row == 1, counts[1], counts[2]))
    own_begin = jnp.where(
        own_row == 0, 0, jnp.where(own_row == 1, counts[0], counts[0] + counts[1])
    )
    at_begin = blk == own_begin
    at_final = blk == own_begin + own_count - 1
    wrap_slot = jnp.where(
        own_count == lengths[0], 1, jnp.where(own_count == lengths[1], 2, 3)
    )
    lag = lag_shift[own_row]
    left_slot = jnp.where(at_begin, wrap_slot, 0)
    right_slot = jnp.where(at_final, wrap_slot, 0)
    left_lag = jnp.where(at_begin, lag, 0)
    right_lag = jnp.where(at_final, instances - lag, 0)

    def others(body):
        def turn(d, carry):
            body(lax.rem(blk + d, n_blk))
            return carry

        lax.fori_loop(1, n_blk, turn, 0)

    def ghost_copy(s, other):
        return pltpu.make_async_remote_copy(
            src_ref=spread.at[other],
            dst_ref=ghosts.at[s],
            send_sem=ghost_send.at[other],
            recv_sem=ghost_recv.at[s],
            device_id=(other, span),
            device_id_type=MESH_ID,
        )

    def face_copy(s, source):
        return pltpu.make_async_remote_copy(
            src_ref=faces.at[s],
            dst_ref=gathered.at[source],
            send_sem=face_send.at[s],
            recv_sem=face_recv.at[source],
            device_id=(source, span),
            device_id_type=MESH_ID,
        )

    own_layer = blk // stride
    is_owner = blk == own_layer * stride

    def each_layer(body):
        def turn(s, carry):
            body(s)
            return carry

        lax.fori_loop(0, span_cells, turn, 0)

    def wait_ghost(s):
        @pl.when(blk != s * stride)
        def _():
            ghost_copy(s, s * stride).wait_recv()

    table = circulant(instances)
    freq = frequency[own_row]
    spectral_weights = [freq * w for w in table]
    damping = [dissipation[own_row, d] for d in range(3)]
    centre = 2.0 * (damping[0] + damping[1] + damping[2])

    def out_copy(s):
        return pltpu.make_async_copy(result.at[:, :, s], out_hbm.at[:, :, s], out_sem.at[s])

    def layers(first, last, fixed, linked):
        def layer(t, carry):
            s = (span_cells - 1) * span + t * (1 - 2 * span)

            def instant(k, inner):
                total, differences = [], []
                for v in range(variables):
                    here = cells[v, k, s + 1]
                    minus, plus, value = {}, {}, None
                    if fixed:
                        minus[2], plus[2] = cells[v, k, s], cells[v, k, s + 2]
                        value = centre * here
                        for n, weight in enumerate(spectral_weights):
                            before = lax.rem(k + instances - n - 1, instances)
                            after = lax.rem(k + n + 1, instances)
                            value = value + weight * (
                                cells[v, before, s + 1] - cells[v, after, s + 1]
                            )
                    if linked:
                        shift = lax.rem(axial + 127 - 2 * (v * instances + k), axial)
                        ghost = pltpu.roll(ghosts[s], shift, 1)
                        k_left = lax.rem(k + left_lag, instances)
                        k_right = lax.rem(k + right_lag, instances)
                        left = left_buf[left_slot, v, k_left, pl.ds(s, 1), :]
                        right = right_buf[right_slot, v, k_right, pl.ds(s, 1), :]
                        minus[0] = jnp.where(sub == 0, left, pltpu.roll(here, 1, 0))
                        plus[0] = jnp.where(
                            sub == pitch - 1, right, pltpu.roll(here, pitch - 1, 0)
                        )
                        minus[1] = jnp.where(lane == 0, ghost, pltpu.roll(here, 1, 1))
                        plus[1] = jnp.where(
                            lane == axial - 1, ghost, pltpu.roll(here, axial - 1, 1)
                        )
                    for d in plus:
                        spread_out = damping[d] * (plus[d] + minus[d])
                        value = -spread_out if value is None else value - spread_out
                    differences.append({d: plus[d] - minus[d] for d in plus})
                    total.append(value)
                pace = step[s]
                for u in range(variables):
                    value = total[u]
                    for v in range(variables):
                        for d, difference in differences[v].items():
                            value = value + half_jacobian[u][d][v] * difference
                    result[u, k, s] = result[u, k, s] - pace * value
                return inner

            lax.fori_loop(0, instances, instant, 0)
            if linked:
                out_copy(s).start()
            return carry

        lax.fori_loop(first, last, layer, 0)

    load_base.wait()
    load_step.wait()
    half_jacobian = [
        [[0.5 * jacobian[own_row, u, d, v] for v in range(variables)] for d in range(3)]
        for u in range(variables)
    ]
    early = 2
    layers(0, early, True, False)

    @pl.when(is_owner)
    def _():
        others(lambda other: face_copy(own_layer, other).wait_recv())
        columns = gathered[...].reshape(n_blk * pitch, axial)
        coefs = jnp.dot(
            analysis[order],
            columns,
            precision=lax.Precision.HIGHEST,
            preferred_element_type=jnp.float32,
        )
        shape = coefs.shape
        term = lax.broadcasted_iota(jnp.int32, shape, 0)
        spot = lax.broadcasted_iota(jnp.int32, shape, 1)
        limit = jnp.where((term // 32) % 2 == 0, mode_count[0], mode_count[1])
        keep = ((term % MODES) < limit) & ((term // 64) == (spot % 2))
        coefs = jnp.where(keep, coefs, 0.0)
        coefs = jnp.where(spot % 2 == 0, pltpu.roll(coefs, axial - 1, 1), pltpu.roll(coefs, 1, 1))
        values = jnp.dot(
            synthesis[order],
            coefs,
            precision=lax.Precision.HIGHEST,
            preferred_element_type=jnp.float32,
        )
        spread[...] = values.reshape(n_blk, pitch, axial)
        ghosts[own_layer] = spread[blk]
        others(lambda other: ghost_copy(own_layer, other).start())

    layers(early, span_cells - 1, True, False)
    for _, receives, side, slot, distance in transfers:

        @pl.when(receives)
        def _(side=side, slot=slot, distance=distance):
            rim_copy(side, slot, -distance).wait_recv()

    each_layer(wait_ghost)
    layers(0, span_cells - 1, False, True)
    span_copy.wait_recv()
    layers(span_cells - 1, span_cells, True, True)

    span_copy.wait_send()
    for sends, _, side, slot, distance in transfers:

        @pl.when(sends)
        def _(side=side, slot=slot, distance=distance):
            rim_copy(side, slot, distance).wait_send()

    def wait_face(s):
        @pl.when(blk != s * stride)
        def _():
            face_copy(s, s * stride).wait_send()

    each_layer(wait_face)

    @pl.when(is_owner)
    def _():
        others(lambda other: ghost_copy(own_layer, other).wait_send())

    each_layer(lambda s: out_copy(s).wait())


def per_device(n_blk, *arrays):
    state_now = arrays[0]
    variables, instances, span_cells, pitch, axial = state_now.shape
    analysis, synthesis = mode_tables(n_blk, pitch)
    rest = list(arrays[3:])
    rest[3] = rest[3].transpose(0, 2, 1, 3)
    rest += [jnp.asarray(analysis), jnp.asarray(synthesis)]
    f32 = jnp.float32
    dma = pltpu.SemaphoreType.DMA
    return pl.pallas_call(
        functools.partial(kernel, n_blk),
        out_shape=jax.ShapeDtypeStruct(state_now.shape, f32),
        in_specs=[pl.BlockSpec(memory_space=pltpu.HBM)] * 11,
        out_specs=pl.BlockSpec(memory_space=pl.ANY),
        scratch_shapes=[
            pltpu.VMEM((variables, instances, span_cells + 2, pitch, axial), f32),
            pltpu.VMEM(state_now.shape, f32),
            pltpu.VMEM((span_cells, pitch, axial), f32),
            pltpu.VMEM((2, variables, instances, span_cells, axial), f32),
            pltpu.VMEM((4, variables, instances, span_cells, axial), f32),
            pltpu.VMEM((4, variables, instances, span_cells, axial), f32),
            pltpu.VMEM((span_cells, pitch, axial), f32),
            pltpu.VMEM((n_blk, pitch, axial), f32),
            pltpu.VMEM((n_blk, pitch, axial), f32),
            pltpu.VMEM((span_cells, pitch, axial), f32),
            *[pltpu.SMEM(a.shape, a.dtype) for a in rest[:6]],
            *[pltpu.VMEM(a.shape, a.dtype) for a in rest[6:]],
            dma((11,)),
            dma((2,)),
            dma((4,)),
            dma((4,)),
            dma((4,)),
            dma((4,)),
            dma((span_cells,)),
            dma((n_blk,)),
            dma((n_blk,)),
            dma((span_cells,)),
            dma((span_cells,)),
        ],
        compiler_params=pltpu.CompilerParams(
            collective_id=0, has_side_effects=True, vmem_limit_bytes=63 * 1024 * 1024
        ),
    )(*arrays[:3], *rest)


def solution(mesh):
    return jax.shard_map(
        functools.partial(per_device, mesh.shape["blk"]),
        mesh=mesh,
        in_specs=(
            P(None, None, "span", "blk", None),
            P(None, None, "span", "blk", None),
            P("span", "blk", None),
            P(),
            P(),
            P(),
            P(),
            P(),
            P(),
        ),
        out_specs=P(None, None, "span", "blk", None),
        check_vma=False,
    )
```

```python
import functools
import itertools

import jax
import jax.numpy as jnp
import numpy as np
from jax import lax
from jax.experimental import pallas as pl
from jax.experimental.pallas import tpu as pltpu
from jax.sharding import PartitionSpec as P

MODES = 16
MESH_ID = pl.DeviceIdType.MESH


def row_orders(blocks):
    widest = blocks // 2 + 1
    lengths = (2, widest, blocks - widest - 2)
    return lengths, [tuple(lengths[i] for i in order) for order in itertools.permutations(range(3))]


def mode_tables(blocks, pitch):
    _, orders = row_orders(blocks)
    columns = blocks * pitch
    modes = np.arange(MODES)
    weight = np.where(modes == 0, 1.0, 2.0)
    analysis = np.zeros((len(orders), 2, 2, 2, MODES, columns))
    synthesis = np.zeros((len(orders), 2, 2, 2, MODES, columns))
    for number, counts in enumerate(orders):
        begin = 0
        for row, count in enumerate(counts):
            width = count * pitch
            own = slice(begin, begin + width)
            phase = modes[:, None] * (2.0 * np.pi * (np.arange(width) + 0.5) / width)[None, :]
            basis = np.stack([np.cos(phase), np.sin(phase)])
            scaled = basis * weight[None, :, None] / width
            if row < 2:
                analysis[number, 0, row, :, :, own] = scaled
                synthesis[number, 1, row, :, :, own] = basis
            if row > 0:
                analysis[number, 1, row - 1, :, :, own] = scaled
                synthesis[number, 0, row - 1, :, :, own] = basis
            begin += width
    analysis = analysis.reshape(len(orders), 8 * MODES, columns)
    synthesis = synthesis.reshape(len(orders), 8 * MODES, columns).transpose(0, 2, 1)
    return analysis.astype(np.float32), synthesis.astype(np.float32)


def circulant(instances):
    offsets = np.arange(1, instances // 2 + 1)
    return [float(x) for x in 0.5 * np.cos(np.pi * offsets) / np.sin(np.pi * offsets / instances)]


def kernel(
    n_blk,
    state_hbm,
    base_hbm,
    step_hbm,
    row_map_hbm,
    lag_shift_hbm,
    mode_count_hbm,
    jacobian_hbm,
    dissipation_hbm,
    frequency_hbm,
    analysis_hbm,
    synthesis_hbm,
    out_hbm,
    cells,
    result,
    step,
    rims,
    left_buf,
    right_buf,
    faces,
    gathered,
    spread,
    ghosts,
    row_map,
    lag_shift,
    mode_count,
    jacobian,
    dissipation,
    frequency,
    analysis,
    synthesis,
    load_sem,
    span_sem,
    left_send,
    left_recv,
    right_send,
    right_recv,
    face_send,
    face_recv,
    ghost_send,
    ghost_recv,
    out_sem,
):
    variables, instances, span_cells, pitch, axial = state_hbm.shape
    lengths, orders = row_orders(n_blk)
    stride = n_blk // span_cells
    blk = lax.axis_index("blk")
    span = lax.axis_index("span")

    load_state = pltpu.make_async_copy(
        state_hbm, cells.at[:, :, pl.ds(1, span_cells)], load_sem.at[0]
    )
    load_base = pltpu.make_async_copy(base_hbm, result, load_sem.at[1])
    load_step = pltpu.make_async_copy(step_hbm, step, load_sem.at[2])
    load_state.start()
    load_base.start()
    load_step.start()
    pairs = [
        (row_map_hbm, row_map),
        (lag_shift_hbm, lag_shift),
        (mode_count_hbm, mode_count),
        (jacobian_hbm, jacobian),
        (dissipation_hbm, dissipation),
        (frequency_hbm, frequency),
        (analysis_hbm, analysis),
        (synthesis_hbm, synthesis),
    ]
    load_rest = [
        pltpu.make_async_copy(source, target, load_sem.at[3 + i])
        for i, (source, target) in enumerate(pairs)
    ]
    for load in load_rest:
        load.start()

    barrier = pltpu.get_barrier_semaphore()
    pl.semaphore_signal(barrier, inc=1, device_id=(blk, 1 - span), device_id_type=MESH_ID)

    def greet(d, carry):
        other = lax.rem(blk + d, n_blk)
        pl.semaphore_signal(barrier, inc=1, device_id=(other, span), device_id_type=MESH_ID)
        return carry

    lax.fori_loop(1, n_blk, greet, 0)

    sub = lax.broadcasted_iota(jnp.int32, (pitch, axial), 0)
    lane = lax.broadcasted_iota(jnp.int32, (pitch, axial), 1)
    pair = lane // 2

    def clear(k, carry):
        for v in range(variables):
            cells[v, k, (span_cells + 1) * span] = jnp.zeros((pitch, axial), jnp.float32)
        return carry

    lax.fori_loop(0, instances, clear, 0)

    span_copy = pltpu.make_async_remote_copy(
        src_ref=state_hbm.at[:, :, (span_cells - 1) * (1 - span)],
        dst_ref=cells.at[:, :, (span_cells + 1) * span],
        send_sem=span_sem.at[0],
        recv_sem=span_sem.at[1],
        device_id=(blk, 1 - span),
        device_id_type=MESH_ID,
    )

    load_state.wait()

    def take(k, tiles):
        tiles = list(tiles)
        for v in range(variables):
            n = v * instances + k
            chosen = pair == n
            for s in range(span_cells):
                tiles[s] = jnp.where(chosen, pltpu.roll(cells[v, k, s + 1], 2 * n + 1, 1), tiles[s])
        return tuple(tiles)

    blank = jnp.zeros((pitch, axial), jnp.float32)
    for s, tile in enumerate(lax.fori_loop(0, instances, take, (blank,) * span_cells)):
        faces[s] = tile

    pl.semaphore_wait(barrier, n_blk)

    def send_layer(s, carry):
        owner = s * stride

        @pl.when(blk == owner)
        def _():
            gathered[blk] = faces[s]

        @pl.when(blk != owner)
        def _():
            pltpu.make_async_remote_copy(
                src_ref=faces.at[s],
                dst_ref=gathered.at[blk],
                send_sem=face_send.at[s],
                recv_sem=face_recv.at[blk],
                device_id=(owner, span),
                device_id_type=MESH_ID,
            ).start()

        return carry

    lax.fori_loop(0, span_cells, send_layer, 0)
    span_copy.start()

    def pack(k, carry):
        for v in range(variables):
            rims[0, v, k] = cells[v, k, pl.ds(1, span_cells), 0, :]
            rims[1, v, k] = cells[v, k, pl.ds(1, span_cells), pitch - 1, :]
        return carry

    lax.fori_loop(0, instances, pack, 0)

    def rim_copy(side, slot, distance):
        other = blk + distance
        buf, send, recv = (
            (right_buf, right_send, right_recv) if side == 0 else (left_buf, left_send, left_recv)
        )
        return pltpu.make_async_remote_copy(
            src_ref=rims.at[side],
            dst_ref=buf.at[slot],
            send_sem=send.at[slot],
            recv_sem=recv.at[slot],
            device_id=(other, span),
            device_id_type=MESH_ID,
        )

    def any_of(values):
        hit = blk == values[0]
        for value in values[1:]:
            hit = hit | (blk == value)
        return hit

    transfers = [
        (blk < n_blk - 1, blk > 0, 1, 0, 1),
        (blk > 0, blk < n_blk - 1, 0, 0, -1),
    ]
    for number, count in enumerate(lengths):
        begins = sorted({sum(o[: o.index(count)]) for o in orders})
        is_begin = any_of(begins)
        is_end = any_of([b + count - 1 for b in begins])
        transfers.append((is_end, is_begin, 1, number + 1, -(count - 1)))
        transfers.append((is_begin, is_end, 0, number + 1, count - 1))
    for sends, _, side, slot, distance in transfers:

        @pl.when(sends)
        def _(side=side, slot=slot, distance=distance):
            rim_copy(side, slot, distance).start()

    for load in load_rest:
        load.wait()

    counts = [0, 0, 0]
    for b in range(n_blk):
        for r in range(3):
            counts[r] = counts[r] + (row_map[b] == r).astype(jnp.int32)
    order = jnp.int32(0)
    for number, o in enumerate(orders):
        same = (counts[0] == o[0]) & (counts[1] == o[1])
        order = order + jnp.where(same, number, 0)
    own_row = row_map[blk]
    own_count = jnp.where(own_row == 0, counts[0], jnp.where(own_row == 1, counts[1], counts[2]))
    own_begin = jnp.where(
        own_row == 0, 0, jnp.where(own_row == 1, counts[0], counts[0] + counts[1])
    )
    at_begin = blk == own_begin
    at_final = blk == own_begin + own_count - 1
    wrap_slot = jnp.where(
        own_count == lengths[0], 1, jnp.where(own_count == lengths[1], 2, 3)
    )
    lag = lag_shift[own_row]
    left_slot = jnp.where(at_begin, wrap_slot, 0)
    right_slot = jnp.where(at_final, wrap_slot, 0)
    left_lag = jnp.where(at_begin, lag, 0)
    right_lag = jnp.where(at_final, instances - lag, 0)

    def others(body):
        def turn(d, carry):
            body(lax.rem(blk + d, n_blk))
            return carry

        lax.fori_loop(1, n_blk, turn, 0)

    def ghost_copy(s, other):
        return pltpu.make_async_remote_copy(
            src_ref=spread.at[other],
            dst_ref=ghosts.at[s],
            send_sem=ghost_send.at[other],
            recv_sem=ghost_recv.at[s],
            device_id=(other, span),
            device_id_type=MESH_ID,
        )

    def face_copy(s, source):
        return pltpu.make_async_remote_copy(
            src_ref=faces.at[s],
            dst_ref=gathered.at[source],
            send_sem=face_send.at[s],
            recv_sem=face_recv.at[source],
            device_id=(source, span),
            device_id_type=MESH_ID,
        )

    own_layer = blk // stride
    is_owner = blk == own_layer * stride

    def each_layer(body):
        def turn(s, carry):
            body(s)
            return carry

        lax.fori_loop(0, span_cells, turn, 0)

    def wait_ghost(s):
        @pl.when(blk != s * stride)
        def _():
            ghost_copy(s, s * stride).wait_recv()

    table = circulant(instances)
    freq = frequency[own_row]
    spectral_weights = [freq * w for w in table]
    damping = [dissipation[own_row, d] for d in range(3)]
    centre = 2.0 * (damping[0] + damping[1] + damping[2])

    def out_copy(s):
        return pltpu.make_async_copy(result.at[:, :, s], out_hbm.at[:, :, s], out_sem.at[s])

    def layers(first, last, fixed, linked):
        def layer(t, carry):
            s = (span_cells - 1) * span + t * (1 - 2 * span)

            def instant(k, inner):
                total, differences = [], []
                for v in range(variables):
                    here = cells[v, k, s + 1]
                    minus, plus, value = {}, {}, None
                    if fixed:
                        minus[2], plus[2] = cells[v, k, s], cells[v, k, s + 2]
                        value = centre * here
                        for n, weight in enumerate(spectral_weights):
                            before = lax.rem(k + instances - n - 1, instances)
                            after = lax.rem(k + n + 1, instances)
                            value = value + weight * (
                                cells[v, before, s + 1] - cells[v, after, s + 1]
                            )
                    if linked:
                        shift = lax.rem(axial + 127 - 2 * (v * instances + k), axial)
                        ghost = pltpu.roll(ghosts[s], shift, 1)
                        k_left = lax.rem(k + left_lag, instances)
                        k_right = lax.rem(k + right_lag, instances)
                        left = left_buf[left_slot, v, k_left, pl.ds(s, 1), :]
                        right = right_buf[right_slot, v, k_right, pl.ds(s, 1), :]
                        minus[0] = jnp.where(sub == 0, left, pltpu.roll(here, 1, 0))
                        plus[0] = jnp.where(
                            sub == pitch - 1, right, pltpu.roll(here, pitch - 1, 0)
                        )
                        minus[1] = jnp.where(lane == 0, ghost, pltpu.roll(here, 1, 1))
                        plus[1] = jnp.where(
                            lane == axial - 1, ghost, pltpu.roll(here, axial - 1, 1)
                        )
                    for d in plus:
                        spread_out = damping[d] * (plus[d] + minus[d])
                        value = -spread_out if value is None else value - spread_out
                    differences.append({d: plus[d] - minus[d] for d in plus})
                    total.append(value)
                pace = step[s]
                for u in range(variables):
                    value = total[u]
                    for v in range(variables):
                        for d, difference in differences[v].items():
                            value = value + half_jacobian[u][d][v] * difference
                    result[u, k, s] = result[u, k, s] - pace * value
                return inner

            lax.fori_loop(0, instances, instant, 0, unroll=3)
            if linked:
                out_copy(s).start()
            return carry

        lax.fori_loop(first, last, layer, 0)

    load_base.wait()
    load_step.wait()
    half_jacobian = [
        [[0.5 * jacobian[own_row, u, d, v] for v in range(variables)] for d in range(3)]
        for u in range(variables)
    ]
    early = 2
    layers(0, early, True, False)

    @pl.when(is_owner)
    def _():
        others(lambda other: face_copy(own_layer, other).wait_recv())
        columns = gathered[...].reshape(n_blk * pitch, axial)
        coefs = jnp.dot(
            analysis[order],
            columns,
            precision=lax.Precision.HIGHEST,
            preferred_element_type=jnp.float32,
        )
        shape = coefs.shape
        term = lax.broadcasted_iota(jnp.int32, shape, 0)
        spot = lax.broadcasted_iota(jnp.int32, shape, 1)
        limit = jnp.where((term // 32) % 2 == 0, mode_count[0], mode_count[1])
        keep = ((term % MODES) < limit) & ((term // 64) == (spot % 2))
        coefs = jnp.where(keep, coefs, 0.0)
        coefs = jnp.where(spot % 2 == 0, pltpu.roll(coefs, axial - 1, 1), pltpu.roll(coefs, 1, 1))
        values = jnp.dot(
            synthesis[order],
            coefs,
            precision=lax.Precision.HIGHEST,
            preferred_element_type=jnp.float32,
        )
        spread[...] = values.reshape(n_blk, pitch, axial)
        ghosts[own_layer] = spread[blk]
        others(lambda other: ghost_copy(own_layer, other).start())

    layers(early, span_cells - 1, True, False)
    for _, receives, side, slot, distance in transfers:

        @pl.when(receives)
        def _(side=side, slot=slot, distance=distance):
            rim_copy(side, slot, -distance).wait_recv()

    each_layer(wait_ghost)
    layers(0, span_cells - 1, False, True)
    span_copy.wait_recv()
    layers(span_cells - 1, span_cells, True, True)

    span_copy.wait_send()
    for sends, _, side, slot, distance in transfers:

        @pl.when(sends)
        def _(side=side, slot=slot, distance=distance):
            rim_copy(side, slot, distance).wait_send()

    def wait_face(s):
        @pl.when(blk != s * stride)
        def _():
            face_copy(s, s * stride).wait_send()

    each_layer(wait_face)

    @pl.when(is_owner)
    def _():
        others(lambda other: ghost_copy(own_layer, other).wait_send())

    each_layer(lambda s: out_copy(s).wait())


def per_device(n_blk, *arrays):
    state_now = arrays[0]
    variables, instances, span_cells, pitch, axial = state_now.shape
    analysis, synthesis = mode_tables(n_blk, pitch)
    rest = list(arrays[3:])
    rest[3] = rest[3].transpose(0, 2, 1, 3)
    rest += [jnp.asarray(analysis), jnp.asarray(synthesis)]
    f32 = jnp.float32
    dma = pltpu.SemaphoreType.DMA
    return pl.pallas_call(
        functools.partial(kernel, n_blk),
        out_shape=jax.ShapeDtypeStruct(state_now.shape, f32),
        in_specs=[pl.BlockSpec(memory_space=pltpu.HBM)] * 11,
        out_specs=pl.BlockSpec(memory_space=pl.ANY),
        scratch_shapes=[
            pltpu.VMEM((variables, instances, span_cells + 2, pitch, axial), f32),
            pltpu.VMEM(state_now.shape, f32),
            pltpu.VMEM((span_cells, pitch, axial), f32),
            pltpu.VMEM((2, variables, instances, span_cells, axial), f32),
            pltpu.VMEM((4, variables, instances, span_cells, axial), f32),
            pltpu.VMEM((4, variables, instances, span_cells, axial), f32),
            pltpu.VMEM((span_cells, pitch, axial), f32),
            pltpu.VMEM((n_blk, pitch, axial), f32),
            pltpu.VMEM((n_blk, pitch, axial), f32),
            pltpu.VMEM((span_cells, pitch, axial), f32),
            *[pltpu.SMEM(a.shape, a.dtype) for a in rest[:6]],
            *[pltpu.VMEM(a.shape, a.dtype) for a in rest[6:]],
            dma((11,)),
            dma((2,)),
            dma((4,)),
            dma((4,)),
            dma((4,)),
            dma((4,)),
            dma((span_cells,)),
            dma((n_blk,)),
            dma((n_blk,)),
            dma((span_cells,)),
            dma((span_cells,)),
        ],
        compiler_params=pltpu.CompilerParams(
            collective_id=0, has_side_effects=True, vmem_limit_bytes=63 * 1024 * 1024
        ),
    )(*arrays[:3], *rest)


def solution(mesh):
    return jax.shard_map(
        functools.partial(per_device, mesh.shape["blk"]),
        mesh=mesh,
        in_specs=(
            P(None, None, "span", "blk", None),
            P(None, None, "span", "blk", None),
            P("span", "blk", None),
            P(),
            P(),
            P(),
            P(),
            P(),
            P(),
        ),
        out_specs=P(None, None, "span", "blk", None),
        check_vma=False,
    )
```
